1024 devices in a mesh: rep: 16 (over z, core), node: 8 (over x), local: 8 (over y).
Axes of the slice: x: 8, y: 8, z: 8, core: 2. Of those that a mesh axis runs over, the one named last changes fastest.
Arguments:
- tokens: bfloat16 [4096, 3584], P(('node', 'local'), 'rep'), may hold values from -6 to 6
- expert_ids: int32 [4096, 4], P(('node', 'local')), may hold values from 0 to 63, as said below
- route_weights: bfloat16 [4096, 4], P(('node', 'local')), may hold values from 0.099609375 to 0.5
- w_gate: bfloat16 [64, 3584, 1024], P(('node', 'local'), 'rep'), may hold values from -0.09375 to 0.09375
- w_up: bfloat16 [64, 3584, 1024], P(('node', 'local'), 'rep'), may hold values from -0.09375 to 0.09375
- w_down: bfloat16 [64, 1024, 3584], P(('node', 'local'), None, 'rep'), may hold values from -0.1875 to 0.1875
- grad_out: bfloat16 [4096, 3584], P(('node', 'local'), 'rep'), may hold values from -6 to 6
Outputs:
- mixed: bfloat16 [4096, 3584], P(('node', 'local'), 'rep')
- token_grad: bfloat16 [4096, 3584], P(('node', 'local'), 'rep')
- gate_weight_grad: bfloat16 [64, 3584, 1024], P(('node', 'local'), 'rep')
- up_weight_grad: bfloat16 [64, 3584, 1024], P(('node', 'local'), 'rep')
- down_weight_grad: bfloat16 [64, 1024, 3584], P(('node', 'local'), None, 'rep')
The draws below stay inside these ranges and needn't reach their ends.
Inputs may be any that keep to these rules, and one draw needn't show every extreme that they name: `expert_ids`: each token names 4 different experts; picks 0 and 1 lie in one node group and picks 2 and 3 in another (expert e lies in group e // 8). The 64 tokens of one device visit every node group exactly 16 times. The tokens of one device name each expert at most 6 times, and in every draw some expert is named exactly 6 times by the tokens of every device.
All inputs are finite; a program needn't handle non-finite values.
Results may differ from the reference program's by a relative error of at most 0.0072.
Values may be sent and summed in bfloat16 or wider, within the bound.
No kernel may reach another device: no remote copies, remote signals or barrier semaphores. Data moves between devices by JAX's collectives and lax.ppermute only.
A program may use at most 32 MiB of HBM per device.

```python
import jax
import jax.numpy as jnp
from jax import lax

D = 3584
FF = 1024
TOPK = 4
TOK = 64
EXPERTS = 64
NODE_HITS = 16
MOST = 6
TOKENS = 4096
N_NODE = 8
N_LOCAL = 8


def draw_expert_ids(key, part):
    key = jax.random.fold_in(key, 7)
    mean_count = 2 * NODE_HITS // N_LOCAL
    spread = MOST - mean_count
    cohorts = TOK // N_NODE
    hot_node = jax.random.randint(jax.random.fold_in(key, 1), (), 0, N_NODE)
    hot_local = jax.random.randint(jax.random.fold_in(key, 2), (), 0, N_LOCAL)
    positions = jnp.arange(N_LOCAL, dtype=jnp.int32)

    def node_lists(node_key, node):
        keys = jax.random.split(node_key, 4)
        order = jax.random.permutation(keys[0], N_LOCAL).astype(jnp.int32)
        where_hot = jnp.sum(jnp.where(order == hot_local, positions, 0))
        moved = jnp.where(positions == 0, hot_local, jnp.where(positions == where_hot, order[0], order))
        order = jnp.where(node == hot_node, moved, order)
        deltas = jax.random.randint(keys[1], (N_LOCAL // 2,), 0, spread + 1)
        deltas = deltas.at[0].set(jnp.where(node == hot_node, spread, deltas[0]))
        signed = jnp.stack([deltas, -deltas], axis=1).reshape(N_LOCAL)
        counts = jnp.zeros((N_LOCAL,), jnp.int32).at[order].set(mean_count + signed)
        running = jnp.cumsum(counts)
        marks = jnp.arange(2 * NODE_HITS, dtype=jnp.int32)
        sorted_locals = jnp.sum((running[None, :] <= marks[:, None]).astype(jnp.int32), axis=1)
        leading = sorted_locals[:NODE_HITS]
        trailing = sorted_locals[NODE_HITS:]
        flips = jax.random.randint(keys[2], (NODE_HITS,), 0, 2)
        pick_first = jnp.where(flips == 1, trailing, leading)
        pick_second = jnp.where(flips == 1, leading, trailing)
        ranks = jax.random.permutation(keys[3], NODE_HITS).astype(jnp.int32)
        return (pick_first[ranks], pick_second[ranks])

    def block_ids(block_key):
        keys = jax.random.split(block_key, 4)
        node_order = jax.random.permutation(keys[0], N_NODE).astype(jnp.int32)
        offsets = jax.random.randint(keys[1], (cohorts,), 1, N_NODE)
        places = jnp.arange(TOK, dtype=jnp.int32)
        cohort = places // N_NODE
        lead_node = node_order[places % N_NODE]
        trail_node = (lead_node + offsets[cohort]) % N_NODE
        lists_first, lists_second = jax.vmap(node_lists)(jax.random.split(keys[2], N_NODE), jnp.arange(N_NODE, dtype=jnp.int32))
        lead_ids = jnp.stack([lead_node * N_LOCAL + lists_first[lead_node, cohort], lead_node * N_LOCAL + lists_second[lead_node, cohort]], axis=1)
        trail_visit = cohorts + cohort
        trail_ids = jnp.stack([trail_node * N_LOCAL + lists_first[trail_node, trail_visit], trail_node * N_LOCAL + lists_second[trail_node, trail_visit]], axis=1)
        chosen = jnp.concatenate([lead_ids, trail_ids], axis=1)
        shuffle = jax.random.permutation(keys[3], TOK)
        return chosen[shuffle]
    blocks = jax.vmap(block_ids)(jax.random.split(key, N_NODE * N_LOCAL))
    return blocks.reshape(TOKENS, TOPK).astype(jnp.int32)


def shard_levels(stream_key, extent, pieces, low, high):
    def one(position, parts):
        heights = jax.random.uniform(jax.random.fold_in(jax.random.fold_in(stream_key, 6), position), (parts,), jnp.float32, low / len(pieces), high / len(pieces))
        return jnp.repeat(jnp.exp(heights), extent[position] // parts).reshape((-1,) + (1,) * (len(extent) - position - 1))

    gain = one(*pieces[0])
    for cut in pieces[1:]:
        gain = gain * one(*cut)
    return gain


def centred(key, dims, width, limit, shards=(), kind=jnp.bfloat16):
    drawn = width * jax.random.normal(key, dims, jnp.float32)
    if shards:
        drawn = drawn * shard_levels(key, dims, shards, -0.22, 0.18)
    return jnp.clip(drawn, -limit, limit).astype(kind)


def setup_inputs(seed: int = 0) -> dict:
    streams_of = jax.random.split(jax.random.key(seed), 8)
    tokens = centred(streams_of[0], (TOKENS, D), 1.0, 6.0, ((0, 64), (1, 16)))
    expert_ids = draw_expert_ids(jax.random.fold_in(streams_of[7], 71), 0)
    route_weights = jnp.clip(0.099609375 + 0.40039062 * jax.random.uniform(streams_of[2], (TOKENS, TOPK), jnp.float32) ** shard_levels(streams_of[2], (TOKENS, TOPK), ((0, 64),), -0.2, 0.2), 0.099609375, 0.5).astype(jnp.bfloat16)
    w_gate = centred(streams_of[3], (EXPERTS, D, FF), D ** -0.5, 0.09375, ((0, 64), (1, 16)))
    w_up = centred(streams_of[4], (EXPERTS, D, FF), D ** -0.5, 0.09375, ((0, 64), (1, 16)))
    w_down = centred(streams_of[5], (EXPERTS, FF, D), FF ** -0.5, 0.1875, ((0, 64), (2, 16)))
    grad_out = centred(streams_of[6], (TOKENS, D), 1.0, 6.0, ((0, 64), (1, 16)))
    return {"tokens": tokens, "expert_ids": expert_ids, "route_weights": route_weights, "w_gate": w_gate, "w_up": w_up, "w_down": w_down, "grad_out": grad_out}


def silu_grads(gate_val, up_val, hidden_grad):
    sigmoid_val = jax.nn.sigmoid(gate_val)
    gate_grad = hidden_grad * up_val * (sigmoid_val * (1.0 + gate_val * (1.0 - sigmoid_val)))
    up_grad = hidden_grad * (gate_val * sigmoid_val)
    return gate_grad.astype(jnp.bfloat16), up_grad.astype(jnp.bfloat16)


def expert_pass(operands):
    token_rows, grad_rows, gate_mat, up_mat, down_mat = operands
    gate_val = jnp.dot(token_rows, gate_mat, preferred_element_type=jnp.float32)
    up_val = jnp.dot(token_rows, up_mat, preferred_element_type=jnp.float32)
    hidden = (jax.nn.silu(gate_val) * up_val).astype(jnp.bfloat16)
    output = jnp.dot(hidden, down_mat, preferred_element_type=jnp.float32).astype(jnp.bfloat16)
    hidden_grad = jnp.dot(grad_rows, down_mat.T, preferred_element_type=jnp.float32)
    gate_grad, up_grad = silu_grads(gate_val, up_val, hidden_grad)
    input_grad = jnp.dot(gate_grad, gate_mat.T, preferred_element_type=jnp.float32) + jnp.dot(up_grad, up_mat.T, preferred_element_type=jnp.float32)
    gate_sum = jnp.dot(token_rows.T, gate_grad, preferred_element_type=jnp.float32).astype(jnp.bfloat16)
    up_sum = jnp.dot(token_rows.T, up_grad, preferred_element_type=jnp.float32).astype(jnp.bfloat16)
    down_sum = jnp.dot(hidden.T, grad_rows, preferred_element_type=jnp.float32).astype(jnp.bfloat16)
    return output, input_grad.astype(jnp.bfloat16), gate_sum, up_sum, down_sum


def group_sums(values):
    paired = (values[:, 0::2] + values[:, 1::2]).astype(jnp.bfloat16)
    paired = lax.optimization_barrier(paired).astype(jnp.float32)
    return jnp.sum(paired, axis=1).astype(jnp.bfloat16)


def reference(tokens, expert_ids, route_weights, w_gate, w_up, w_down, grad_out):
    depth = EXPERTS * MOST
    flat_ids = expert_ids.reshape(EXPERTS, TOK * TOPK)
    labels = jnp.arange(EXPERTS, dtype=jnp.int32)
    onehot = (flat_ids[:, :, None] == labels[None, None, :]).astype(jnp.int32)
    before = jnp.cumsum(onehot, axis=1) - onehot
    slot_index = jnp.sum(before * onehot, axis=2).reshape(TOKENS, TOPK)
    source = (jnp.arange(TOKENS, dtype=jnp.int32) // TOK)[:, None]
    row_index = (expert_ids * depth + source * MOST + slot_index).reshape(-1).astype(jnp.int32)
    token_index = jnp.repeat(jnp.arange(TOKENS, dtype=jnp.int32), TOPK)
    token_rows = jnp.zeros((EXPERTS * depth, D), tokens.dtype).at[row_index].set(tokens[token_index])
    weights = route_weights.astype(jnp.float32)
    scaled = (weights[:, :, None] * grad_out.astype(jnp.float32)[:, None, :]).astype(jnp.bfloat16)
    grad_rows = jnp.zeros((EXPERTS * depth, D), scaled.dtype).at[row_index].set(scaled.reshape(-1, D))
    outputs, input_rows, gate_sum, up_sum, down_sum = lax.map(expert_pass, (token_rows.reshape(EXPERTS, depth, D), grad_rows.reshape(EXPERTS, depth, D), w_gate, w_up, w_down))
    picked = outputs.reshape(-1, D)[row_index].reshape(TOKENS, TOPK, D).astype(jnp.float32)
    mixed = group_sums(weights[:, :, None] * picked)
    returned = input_rows.reshape(-1, D)[row_index].reshape(TOKENS, TOPK, D).astype(jnp.float32)
    token_grad = group_sums(returned)
    return mixed, token_grad, gate_sum, up_sum, down_sum
```

```python
import functools

import jax
import jax.numpy as jnp
from jax import lax
from jax.experimental import pallas as pl
from jax.experimental.pallas import tpu as pltpu
from jax.sharding import PartitionSpec as P

BF16 = jnp.bfloat16
F32 = jnp.float32
SLOTS = 8
LIMIT = 40 * 1024 * 1024

NN = (((1,), (0,)), ((), ()))
NT = (((1,), (1,)), ((), ()))
TN = (((0,), (0,)), ((), ()))


def mm(a, b, dims=NN):
    return lax.dot_general(a, b, dims, preferred_element_type=F32)


def vmem(count):
    return [pl.BlockSpec(memory_space=pltpu.VMEM)] * count


def call(kernel, outs, *args, scalars=0, scratch=()):
    specs = [pl.BlockSpec(memory_space=pltpu.SMEM)] * scalars + vmem(len(args) - scalars)
    return pl.pallas_call(
        kernel,
        out_shape=[jax.ShapeDtypeStruct(shape, dtype) for shape, dtype in outs],
        in_specs=specs,
        out_specs=vmem(len(outs)),
        scratch_shapes=list(scratch),
        compiler_params=pltpu.CompilerParams(vmem_limit_bytes=LIMIT),
    )(*args)


def pack_kernel(core_ref, gate_ref, up_ref, down_ref, own_ref, send_ref):
    width, hidden = gate_ref.shape
    half = hidden // 2
    quarter = half // 2
    for ref, which in ((own_ref, core_ref[0]), (send_ref, 1 - core_ref[0])):
        start = pl.multiple_of(which * half, half)
        ref[0:width, :] = gate_ref[:, pl.ds(start, half)]
        ref[width : 2 * width, :] = up_ref[:, pl.ds(start, half)]
        ref[2 * width :, :] = jnp.zeros((quarter, half), BF16)
        ref[2 * width :, 0:width] = down_ref[pl.ds(start, quarter), :]
        ref[2 * width :, quarter : quarter + width] = down_ref[
            pl.ds(pl.multiple_of(start + quarter, quarter), quarter), :
        ]


def route_kernel(ids_ref, weight_ref, token_ref, grad_ref, send_ref, mark_ref, scale_ref):
    tokens, picks = ids_ref.shape
    width = token_ref.shape[1]
    rows = mark_ref.shape[0]
    experts = rows // SLOTS
    side = send_ref.shape[1] // 2
    row_i = lax.broadcasted_iota(jnp.int32, (tokens, tokens), 0)
    col_i = lax.broadcasted_iota(jnp.int32, (tokens, tokens), 1)
    eye = (row_i == col_i).astype(F32)
    earlier = (row_i < col_i).astype(F32)
    ids = mm(ids_ref[...].astype(F32), eye, TN)
    weights = mm(weight_ref[...].astype(F32), eye, TN)
    expert_i = lax.broadcasted_iota(jnp.int32, (experts, tokens), 0).astype(F32)
    row_all = lax.broadcasted_iota(jnp.int32, (rows, tokens), 0).astype(F32)
    before = jnp.zeros((experts, 1), F32)
    marks, scales = [], []
    for pick in range(picks):
        hit = (expert_i == ids[pick : pick + 1, :]).astype(F32)
        count = mm(hit, earlier) + before
        slot = jnp.sum(hit * count, axis=0, keepdims=True)
        before = before + jnp.sum(hit, axis=1, keepdims=True)
        found = row_all == ids[pick : pick + 1, :] * SLOTS + slot
        marks.append(jnp.where(found, 1.0, 0.0))
        scales.append(jnp.where(found, weights[pick : pick + 1, :], 0.0))
    mark = jnp.concatenate([marks[0] + marks[1], marks[2] + marks[3]], axis=1).astype(BF16)
    scale = jnp.concatenate([scales[0] + scales[1], scales[2] + scales[3]], axis=1).astype(BF16)
    mark_ref[...] = mark
    scale_ref[...] = scale
    twice = lambda ref: jnp.concatenate([ref[...], ref[...]], axis=0)
    send_ref[...] = jnp.zeros_like(send_ref)
    send_ref[:, 0:width] = mm(mark, twice(token_ref)).astype(BF16)
    send_ref[:, side : side + width] = mm(scale, twice(grad_ref)).astype(BF16)


def slot_matrix(rows, kept, turned):
    sources = rows // SLOTS
    shape = (rows, kept) if turned else (kept, rows)
    small = lax.broadcasted_iota(jnp.int32, shape, 1 if turned else 0)
    large = lax.broadcasted_iota(jnp.int32, shape, 0 if turned else 1)
    return (lax.rem(small, sources) * SLOTS + small // sources == large).astype(BF16)


def sums_kernel(core_ref, rows_ref, own_ref, other_ref, sum_ref, kept_ref):
    rows, wide = rows_ref.shape[1:]
    kept = sum_ref.shape[0]
    side = wide // 2
    half = own_ref.shape[1]
    quarter = half // 2
    width = (own_ref.shape[0] - quarter) // 2
    pack = slot_matrix(rows, kept, False)
    mine = mm(pack, rows_ref[core_ref[0]]).astype(BF16)
    kept_ref[...] = mine
    theirs = mm(pack, rows_ref[1 - core_ref[0]]).astype(BF16)
    x_own, y_own = mine[:, 0:width], mine[:, side : side + width]
    x_other, y_other = theirs[:, 0:width], theirs[:, side : side + width]
    for part in range(2):
        lo = part * width
        sum_ref[:, part * half : (part + 1) * half] = mm(
            x_own, own_ref[lo : lo + width, :]
        ) + mm(x_other, other_ref[lo : lo + width, :])
    for part in range(2):
        lo = part * quarter
        sum_ref[:, 2 * half + lo : 2 * half + lo + quarter] = mm(
            y_own, own_ref[2 * width :, lo : lo + width], NT
        ) + mm(y_other, other_ref[2 * width :, lo : lo + width], NT)


def hidden_kernel(sum_ref, out_ref):
    half = sum_ref.shape[1] // 3
    gate = sum_ref[:, 0:half]
    up = sum_ref[:, half : 2 * half]
    back = sum_ref[:, 2 * half :]
    sig = jax.nn.sigmoid(gate)
    out_ref[:, 0:half] = (gate * sig * up).astype(BF16)
    out_ref[:, half : 2 * half] = (back * up * (sig * (1.0 + gate * (1.0 - sig)))).astype(BF16)
    out_ref[:, 2 * half :] = (back * (gate * sig)).astype(BF16)


def products_kernel(
    all_ref, kept_ref, gate_ref, up_ref, down_ref,
    send_ref, gate_sum_ref, up_sum_ref, down_sum_ref, hid_ref, dgate_ref, dup_ref, out_ref,
):
    kept, wide = kept_ref.shape
    side = wide // 2
    width, hidden = gate_ref.shape
    half = hidden // 2
    block = all_ref.shape[0] // 16
    for index in range(16):
        chip, core = index // 2, index % 2
        for part, ref in enumerate((hid_ref, dgate_ref, dup_ref)):
            ref[chip * block : (chip + 1) * block, core * half : (core + 1) * half] = all_ref[
                index * block : (index + 1) * block, part * half : (part + 1) * half
            ]
    out_ref[...] = jnp.zeros_like(out_ref)
    out_ref[:, 0:width] = mm(hid_ref[...], down_ref[...]).astype(BF16)
    out_ref[:, side : side + width] = (
        mm(dgate_ref[...], gate_ref[...], NT) + mm(dup_ref[...], up_ref[...], NT)
    ).astype(BF16)
    send_ref[...] = mm(slot_matrix(send_ref.shape[0], kept, True), out_ref[...]).astype(BF16)
    token_rows = kept_ref[:, 0:width]
    grad_rows = kept_ref[:, side : side + width]
    gate_sum_ref[...] = mm(token_rows, dgate_ref[...], TN).astype(BF16)
    up_sum_ref[...] = mm(token_rows, dup_ref[...], TN).astype(BF16)
    down_sum_ref[...] = mm(hid_ref[...], grad_rows, TN).astype(BF16)


def combine_kernel(back_ref, mark_ref, scale_ref, mixed_ref, token_grad_ref):
    tokens, width = mixed_ref.shape
    side = back_ref.shape[1] // 2
    for ref, marks, lo in ((mixed_ref, scale_ref, 0), (token_grad_ref, mark_ref, side)):
        parts = mm(marks[...], back_ref[:, lo : lo + width], TN).astype(BF16).astype(F32)
        ref[...] = (parts[0:tokens] + parts[tokens:]).astype(BF16)


def shards(tokens, expert_ids, route_weights, w_gate, w_up, w_down, grad_out):
    count, width = tokens.shape
    rep = lax.axis_size("rep")
    experts = lax.axis_size("node") * lax.axis_size("local")
    hidden = w_gate.shape[2]
    half, quarter = hidden // 2, hidden // 4
    side = -(-width // 128) * 128
    node_hits = 2 * count // lax.axis_size("node")
    mean_count = 2 * node_hits // lax.axis_size("local")
    depth = min(mean_count + max(mean_count // 2, 1), node_hits)
    kept = experts * depth
    rows = experts * SLOTS
    pairs = [[2 * i, 2 * i + 1] for i in range(rep // 2)]
    lines = [list(range(c, rep, 2)) for c in range(2)]
    core = (lax.axis_index("rep") % 2).astype(jnp.int32).reshape(1)
    gate_mat, up_mat, down_mat = w_gate[0], w_up[0], w_down[0]

    packed = ((2 * width + quarter, half), BF16)
    own, give = call(
        pack_kernel, [packed, packed], core, gate_mat, up_mat, down_mat, scalars=1
    )
    other = lax.ppermute(give, "rep", [(i, i ^ 1) for i in range(rep)])
    expert_ids, own = lax.optimization_barrier((expert_ids, own))
    send, mark, scale = call(
        route_kernel,
        [((rows, 2 * side), BF16), ((rows, 2 * count), BF16), ((rows, 2 * count), BF16)],
        expert_ids, route_weights, tokens, grad_out,
    )
    arrived = lax.all_to_all(
        send.reshape(experts, SLOTS, 2 * side), ("node", "local"), 0, 0, tiled=True
    )
    both = lax.all_gather(
        arrived.reshape(rows, 2 * side), "rep", axis=0, tiled=True, axis_index_groups=pairs
    )
    sums, kept_rows = call(
        sums_kernel,
        [((kept, 3 * half), F32), ((kept, 2 * side), BF16)],
        core, both.reshape(2, rows, 2 * side), own, other, scalars=1,
    )
    sums = lax.psum_scatter(
        sums, "rep", scatter_dimension=0, tiled=True, axis_index_groups=lines
    )
    (piece,) = call(hidden_kernel, [(sums.shape, BF16)], sums)
    whole = lax.all_gather(piece, "rep", axis=0, tiled=True)
    matrix = ((kept, hidden), BF16)
    send_back, gate_sum, up_sum, down_sum = call(
        products_kernel,
        [
            ((rows, 2 * side), BF16),
            (gate_mat.shape, BF16),
            (up_mat.shape, BF16),
            (down_mat.shape, BF16),
        ],
        whole, kept_rows, gate_mat, up_mat, down_mat,
        scratch=[pltpu.VMEM(*matrix)] * 3 + [pltpu.VMEM((kept, 2 * side), BF16)],
    )
    back = lax.all_to_all(
        send_back.reshape(experts, SLOTS, 2 * side), ("node", "local"), 0, 0, tiled=True
    )
    mixed, token_grad = call(
        combine_kernel,
        [(tokens.shape, BF16), (tokens.shape, BF16)],
        back.reshape(rows, 2 * side), mark, scale,
    )
    return (mixed, token_grad, gate_sum[None], up_sum[None], down_sum[None])


def solution(mesh):
    return jax.shard_map(
        shards,
        mesh=mesh,
        in_specs=(
            P(("node", "local"), "rep"),
            P(("node", "local"), None),
            P(("node", "local"), None),
            P(("node", "local"), "rep", None),
            P(("node", "local"), "rep", None),
            P(("node", "local"), None, "rep"),
            P(("node", "local"), "rep"),
        ),
        out_specs=(
            P(("node", "local"), "rep"),
            P(("node", "local"), "rep"),
            P(("node", "local"), "rep", None),
            P(("node", "local"), "rep", None),
            P(("node", "local"), None, "rep"),
        ),
        check_vma=False,
    )
```

```python
import jax
import jax.numpy as jnp
from jax import lax
from jax.experimental import pallas as pl
from jax.experimental.pallas import tpu as pltpu
from jax.sharding import PartitionSpec as P

BF16 = jnp.bfloat16
F32 = jnp.float32
SLOTS = 8
LIMIT = 40 * 1024 * 1024

NN = (((1,), (0,)), ((), ()))
NT = (((1,), (1,)), ((), ()))
TN = (((0,), (0,)), ((), ()))


def mm(a, b, dims=NN):
    return lax.dot_general(a, b, dims, preferred_element_type=F32)


def vmem(count):
    return [pl.BlockSpec(memory_space=pltpu.VMEM)] * count


def call(kernel, outs, *args, scalars=0, scratch=()):
    specs = [pl.BlockSpec(memory_space=pltpu.SMEM)] * scalars + vmem(len(args) - scalars)
    return pl.pallas_call(
        kernel,
        out_shape=[jax.ShapeDtypeStruct(shape, dtype) for shape, dtype in outs],
        in_specs=specs,
        out_specs=vmem(len(outs)),
        scratch_shapes=list(scratch),
        compiler_params=pltpu.CompilerParams(vmem_limit_bytes=LIMIT),
    )(*args)


def pack_kernel(core_ref, gate_ref, up_ref, down_ref, own_ref, send_ref):
    width, hidden = gate_ref.shape
    half = hidden // 2
    for ref, which in ((own_ref, core_ref[0]), (send_ref, 1 - core_ref[0])):
        start = pl.multiple_of(which * half, half)
        for part, mat_ref in enumerate((gate_ref, up_ref, down_ref)):
            ref[part * width : (part + 1) * width, :] = mat_ref[:, pl.ds(start, half)]


def route_kernel(ids_ref, weight_ref, token_ref, grad_ref, send_ref, mark_ref, scale_ref):
    picks, tokens = ids_ref.shape
    width = token_ref.shape[1]
    rows = mark_ref.shape[0]
    experts = rows // SLOTS
    side = send_ref.shape[1] // 2
    row_i = lax.broadcasted_iota(jnp.int32, (tokens, tokens), 0)
    col_i = lax.broadcasted_iota(jnp.int32, (tokens, tokens), 1)
    earlier = (row_i < col_i).astype(F32)
    ids = ids_ref[...].astype(F32)
    weights = weight_ref[...].astype(F32)
    expert_i = lax.broadcasted_iota(jnp.int32, (experts, tokens), 0).astype(F32)
    row_all = lax.broadcasted_iota(jnp.int32, (rows, tokens), 0).astype(F32)
    before = jnp.zeros((experts, 1), F32)
    marks, scales = [], []
    for pick in range(picks):
        hit = (expert_i == ids[pick : pick + 1, :]).astype(F32)
        count = mm(hit, earlier) + before
        slot = jnp.sum(hit * count, axis=0, keepdims=True)
        before = before + jnp.sum(hit, axis=1, keepdims=True)
        found = row_all == ids[pick : pick + 1, :] * SLOTS + slot
        marks.append(jnp.where(found, 1.0, 0.0))
        scales.append(jnp.where(found, weights[pick : pick + 1, :], 0.0))
    mark = jnp.concatenate([marks[0] + marks[1], marks[2] + marks[3]], axis=1).astype(BF16)
    scale = jnp.concatenate([scales[0] + scales[1], scales[2] + scales[3]], axis=1).astype(BF16)
    mark_ref[...] = mark
    scale_ref[...] = scale
    twice = lambda ref: jnp.concatenate([ref[...], ref[...]], axis=0)
    send_ref[...] = jnp.zeros_like(send_ref)
    send_ref[:, 0:width] = mm(mark, twice(token_ref)).astype(BF16)
    send_ref[:, side : side + width] = mm(scale, twice(grad_ref)).astype(BF16)


def slot_matrix(rows, kept, turned):
    sources = rows // SLOTS
    shape = (rows, kept) if turned else (kept, rows)
    small = lax.broadcasted_iota(jnp.int32, shape, 1 if turned else 0)
    large = lax.broadcasted_iota(jnp.int32, shape, 0 if turned else 1)
    return (lax.rem(small, sources) * SLOTS + small // sources == large).astype(BF16)


def sums_kernel(mine_ref, theirs_ref, own_ref, other_ref, sum_ref, kept_ref):
    rows, wide = mine_ref.shape
    kept = sum_ref.shape[0]
    side = wide // 2
    half = own_ref.shape[1]
    width = own_ref.shape[0] // 3
    pack = slot_matrix(rows, kept, False)
    mine = mm(pack, mine_ref[...]).astype(BF16)
    kept_ref[...] = mine
    theirs = mm(pack, theirs_ref[...]).astype(BF16)
    for part, lo in enumerate((0, 0, side)):
        block = slice(part * width, (part + 1) * width)
        sum_ref[:, part * half : (part + 1) * half] = (
            mm(mine[:, lo : lo + width], own_ref[block, :])
            + mm(theirs[:, lo : lo + width], other_ref[block, :])
        ).astype(BF16)


def hidden_kernel(sum_ref, hid_ref, dgate_ref, dup_ref):
    half = sum_ref.shape[2] // 3
    total = lambda part: jnp.sum(
        sum_ref[:, :, part * half : (part + 1) * half].astype(F32), axis=0
    )
    gate, up, back = total(0), total(1), total(2)
    sig = jax.nn.sigmoid(gate)
    hid = (gate * sig * up).astype(BF16)
    for peer in range(hid_ref.shape[0]):
        hid_ref[peer] = hid
    dgate_ref[...] = (back * up * (sig * (1.0 + gate * (1.0 - sig)))).astype(BF16)
    dup_ref[...] = (back * (gate * sig)).astype(BF16)


def rows_kernel(
    core_ref, own_ref, other_ref, dgates_ref, dups_ref, gate_ref, up_ref, down_ref,
    send_ref, hid_ref, dgate_ref, dup_ref, out_ref,
):
    kept, hidden = hid_ref.shape
    half = hidden // 2
    width = gate_ref.shape[0]
    side = out_ref.shape[1] // 2
    block = dgates_ref.shape[0] // 16
    for ref, which in ((own_ref, core_ref[0]), (other_ref, 1 - core_ref[0])):
        hid_ref[:, pl.ds(pl.multiple_of(which * half, half), half)] = ref[...]
    for index in range(16):
        chip, core = index // 2, index % 2
        for ref, piece_ref in ((dgate_ref, dgates_ref), (dup_ref, dups_ref)):
            ref[chip * block : (chip + 1) * block, core * half : (core + 1) * half] = piece_ref[
                index * block : (index + 1) * block, :
            ]
    out_ref[...] = jnp.zeros_like(out_ref)
    out_ref[:, 0:width] = mm(hid_ref[...], down_ref[...], NT).astype(BF16)
    out_ref[:, side : side + width] = (
        mm(dgate_ref[...], gate_ref[...], NT) + mm(dup_ref[...], up_ref[...], NT)
    ).astype(BF16)
    send_ref[...] = mm(slot_matrix(send_ref.shape[0], kept, True), out_ref[...]).astype(BF16)


def weights_kernel(
    kept_ref, hid_ref, dgate_ref, dup_ref, gate_sum_ref, up_sum_ref, down_sum_ref
):
    width = gate_sum_ref.shape[0]
    side = kept_ref.shape[1] // 2
    token_rows = kept_ref[:, 0:width]
    grad_rows = kept_ref[:, side : side + width]
    gate_sum_ref[...] = mm(token_rows, dgate_ref[...], TN).astype(BF16)
    up_sum_ref[...] = mm(token_rows, dup_ref[...], TN).astype(BF16)
    down_sum_ref[...] = mm(grad_rows, hid_ref[...], TN).astype(BF16)


def combine_kernel(back_ref, mark_ref, scale_ref, mixed_ref, token_grad_ref):
    tokens, width = mixed_ref.shape
    side = back_ref.shape[1] // 2
    for ref, marks, lo in ((mixed_ref, scale_ref, 0), (token_grad_ref, mark_ref, side)):
        parts = mm(marks[...], back_ref[:, lo : lo + width], TN).astype(BF16).astype(F32)
        ref[...] = (parts[0:tokens] + parts[tokens:]).astype(BF16)


def shards(tokens, expert_ids, route_weights, w_gate, w_up, w_down, grad_out):
    count, width = tokens.shape
    rep = lax.axis_size("rep")
    experts = lax.axis_size("node") * lax.axis_size("local")
    hidden = w_gate.shape[2]
    half = hidden // 2
    side = -(-width // 128) * 128
    node_hits = 2 * count // lax.axis_size("node")
    mean_count = 2 * node_hits // lax.axis_size("local")
    depth = min(mean_count + max(mean_count // 2, 1), node_hits)
    kept = experts * depth
    rows = experts * SLOTS
    lines = [list(range(c, rep, 2)) for c in range(2)]
    chips = rep // 2
    swap = [(i, i ^ 1) for i in range(rep)]
    core = (lax.axis_index("rep") % 2).astype(jnp.int32).reshape(1)
    gate_mat, up_mat, down_mat = w_gate[0], w_up[0], w_down[0].T

    send, mark, scale = call(
        route_kernel,
        [((rows, 2 * side), BF16), ((rows, 2 * count), BF16), ((rows, 2 * count), BF16)],
        expert_ids.T, route_weights.T, tokens, grad_out,
    )
    mine = lax.all_to_all(
        send.reshape(experts, SLOTS, 2 * side), ("node", "local"), 0, 0, tiled=True
    ).reshape(rows, 2 * side)
    packed = ((3 * width, half), BF16)
    own, give = call(
        pack_kernel, [packed, packed], core, gate_mat, up_mat, down_mat, scalars=1
    )
    other = lax.ppermute(give, "rep", swap)
    theirs = lax.ppermute(mine, "rep", swap)
    sums, kept_rows = call(
        sums_kernel,
        [((kept, 3 * half), BF16), ((kept, 2 * side), BF16)],
        mine, theirs, own, other,
    )
    sums = lax.all_to_all(
        sums.reshape(chips, kept // chips, 3 * half),
        "rep", 0, 0, tiled=True, axis_index_groups=lines,
    )
    piece = ((kept // chips, half), BF16)
    hid, dgate, dup = call(
        hidden_kernel, [((chips,) + piece[0], BF16), piece, piece], sums
    )
    hid_own = lax.all_to_all(
        hid, "rep", 0, 0, tiled=True, axis_index_groups=lines
    ).reshape(kept, half)
    dgates = lax.all_gather(dgate, "rep", axis=0, tiled=True)
    dgates, dup, hid_own = lax.optimization_barrier((dgates, dup, hid_own))
    hid_other = lax.ppermute(hid_own, "rep", swap)
    dups = lax.all_gather(dup, "rep", axis=0, tiled=True)
    matrix = ((kept, hidden), BF16)
    send_back, hid, dgate, dup = call(
        rows_kernel,
        [((rows, 2 * side), BF16), matrix, matrix, matrix],
        core, hid_own, hid_other, dgates, dups, gate_mat, up_mat, down_mat,
        scalars=1,
        scratch=[pltpu.VMEM((kept, 2 * side), BF16)],
    )
    back = lax.all_to_all(
        send_back.reshape(experts, SLOTS, 2 * side), ("node", "local"), 0, 0, tiled=True
    )
    grads = ((width, hidden), BF16)
    gate_sum, up_sum, down_sum = call(
        weights_kernel, [grads, grads, grads], kept_rows, hid, dgate, dup
    )
    mixed, token_grad = call(
        combine_kernel,
        [(tokens.shape, BF16), (tokens.shape, BF16)],
        back.reshape(rows, 2 * side), mark, scale,
    )
    return (mixed, token_grad, gate_sum[None], up_sum[None], down_sum.T[None])


def solution(mesh):
    return jax.shard_map(
        shards,
        mesh=mesh,
        in_specs=(
            P(("node", "local"), "rep"),
            P(("node", "local"), None),
            P(("node", "local"), None),
            P(("node", "local"), "rep", None),
            P(("node", "local"), "rep", None),
            P(("node", "local"), None, "rep"),
            P(("node", "local"), "rep"),
        ),
        out_specs=(
            P(("node", "local"), "rep"),
            P(("node", "local"), "rep"),
            P(("node", "local"), "rep", None),
            P(("node", "local"), "rep", None),
            P(("node", "local"), None, "rep"),
        ),
        check_vma=False,
    )
```

```python
import jax
import jax.numpy as jnp
from jax import lax
from jax.experimental import pallas as pl
from jax.experimental.pallas import tpu as pltpu
from jax.sharding import PartitionSpec as P

BF16 = jnp.bfloat16
F32 = jnp.float32
SLOTS = 8
LIMIT = 40 * 1024 * 1024

NN = (((1,), (0,)), ((), ()))
NT = (((1,), (1,)), ((), ()))
TN = (((0,), (0,)), ((), ()))


def mm(a, b, dims=NN):
    return lax.dot_general(a, b, dims, preferred_element_type=F32)


def call(kernel, outs, *args, scalars=0, far=(), far_in=False, scratch=(), limit=LIMIT):
    near = pl.BlockSpec(memory_space=pltpu.VMEM)
    away = pl.BlockSpec(memory_space=pl.ANY)
    specs = [pl.BlockSpec(memory_space=pltpu.SMEM)] * scalars
    specs += [away if far_in else near] * (len(args) - scalars)
    return pl.pallas_call(
        kernel,
        out_shape=[jax.ShapeDtypeStruct(shape, dtype) for shape, dtype in outs],
        in_specs=specs,
        out_specs=[away if i in far else near for i in range(len(outs))],
        scratch_shapes=list(scratch),
        compiler_params=pltpu.CompilerParams(vmem_limit_bytes=limit),
    )(*args)


def pack_kernel(core_ref, gate_ref, up_ref, down_ref, own_ref, send_ref):
    width, hidden = gate_ref.shape
    half = hidden // 2
    for ref, which in ((own_ref, core_ref[0]), (send_ref, 1 - core_ref[0])):
        start = pl.multiple_of(which * half, half)
        for part, mat_ref in enumerate((gate_ref, up_ref, down_ref)):
            ref[part * width : (part + 1) * width, :] = mat_ref[:, pl.ds(start, half)]


def route_kernel(
    ids_in, weight_in, token_in, grad_in, send_out, mark_out, scale_out,
    ids_ref, weight_ref, token_ref, grad_ref, send_ref, mark_ref, scale_ref, sems,
):
    pairs = (
        (ids_in, ids_ref), (weight_in, weight_ref), (token_in, token_ref), (grad_in, grad_ref),
        (mark_ref, mark_out), (scale_ref, scale_out), (send_ref, send_out),
    )
    copies = [pltpu.make_async_copy(*pair, sems.at[i]) for i, pair in enumerate(pairs)]
    for copy in copies[:4]:
        copy.start()
    copies[0].wait()
    copies[1].wait()
    picks, tokens = ids_ref.shape
    width = token_ref.shape[1]
    rows = mark_ref.shape[0]
    experts = rows // SLOTS
    side = send_ref.shape[1] // 2
    row_i = lax.broadcasted_iota(jnp.int32, (tokens, tokens), 0)
    col_i = lax.broadcasted_iota(jnp.int32, (tokens, tokens), 1)
    earlier = (row_i < col_i).astype(F32)
    ids = ids_ref[...].astype(F32)
    weights = weight_ref[...].astype(F32)
    expert_i = lax.broadcasted_iota(jnp.int32, (experts, tokens), 0).astype(F32)
    row_all = lax.broadcasted_iota(jnp.int32, (rows, tokens), 0).astype(F32)
    before = jnp.zeros((experts, 1), F32)
    marks, scales = [], []
    for pick in range(picks):
        hit = (expert_i == ids[pick : pick + 1, :]).astype(F32)
        count = mm(hit, earlier) + before
        slot = jnp.sum(hit * count, axis=0, keepdims=True)
        before = before + jnp.sum(hit, axis=1, keepdims=True)
        found = row_all == ids[pick : pick + 1, :] * SLOTS + slot
        marks.append(jnp.where(found, 1.0, 0.0))
        scales.append(jnp.where(found, weights[pick : pick + 1, :], 0.0))
    mark = jnp.concatenate([marks[0] + marks[1], marks[2] + marks[3]], axis=1).astype(BF16)
    scale = jnp.concatenate([scales[0] + scales[1], scales[2] + scales[3]], axis=1).astype(BF16)
    mark_ref[...] = mark
    scale_ref[...] = scale
    copies[4].start()
    copies[5].start()
    copies[2].wait()
    copies[3].wait()
    twice = lambda ref: jnp.concatenate([ref[...], ref[...]], axis=0)
    send_ref[...] = jnp.zeros_like(send_ref)
    send_ref[:, 0:width] = mm(mark, twice(token_ref)).astype(BF16)
    send_ref[:, side : side + width] = mm(scale, twice(grad_ref)).astype(BF16)
    copies[6].start()
    for copy in copies[4:]:
        copy.wait()


def slot_matrix(rows, kept, turned):
    sources = rows // SLOTS
    shape = (rows, kept) if turned else (kept, rows)
    small = lax.broadcasted_iota(jnp.int32, shape, 1 if turned else 0)
    large = lax.broadcasted_iota(jnp.int32, shape, 0 if turned else 1)
    return (lax.rem(small, sources) * SLOTS + small // sources == large).astype(BF16)


def sums_kernel(
    mine_ref, theirs_ref, own_ref, other_ref, sum_ref, kept_out, kept_ref, sem
):
    rows, wide = mine_ref.shape
    kept = sum_ref.shape[0]
    side = wide // 2
    half = own_ref.shape[1]
    width = own_ref.shape[0] // 3
    pack = slot_matrix(rows, kept, False)
    mine = mm(pack, mine_ref[...]).astype(BF16)
    kept_ref[...] = mine
    copy = pltpu.make_async_copy(kept_ref, kept_out, sem)
    copy.start()
    theirs = mm(pack, theirs_ref[...]).astype(BF16)
    for part, lo in enumerate((0, 0, side)):
        block = slice(part * width, (part + 1) * width)
        sum_ref[:, part * half : (part + 1) * half] = (
            mm(mine[:, lo : lo + width], own_ref[block, :])
            + mm(theirs[:, lo : lo + width], other_ref[block, :])
        ).astype(BF16)
    copy.wait()


def power_of_two(exponent):
    left = jnp.abs(exponent)
    result = jnp.ones_like(exponent)
    for bit in (64, 32, 16, 8, 4, 2, 1):
        taken = left >= bit
        step = jnp.where(exponent >= 0, 2.0**bit, 2.0**-bit)
        result = jnp.where(taken, result * step, result)
        left = jnp.where(taken, left - bit, left)
    return result


def hidden_kernel(sum_ref, out_ref):
    half = sum_ref.shape[2] // 3
    total = lambda part: jnp.sum(
        sum_ref[:, :, part * half : (part + 1) * half].astype(F32), axis=0
    )
    gate, up, back = total(0), total(1), total(2)
    sig = jax.nn.sigmoid(gate)
    values = (
        gate * sig * up,
        back * up * (sig * (1.0 + gate * (1.0 - sig))),
        back * (gate * sig),
    )
    lane = lax.broadcasted_iota(jnp.int32, (gate.shape[0], 128), 1)
    exponents = jnp.zeros(lane.shape, F32)
    for part, value in enumerate(values):
        value = value.astype(BF16).astype(F32)
        peak = jnp.max(jnp.abs(value), axis=1, keepdims=True)
        exponent = jnp.ceil(jnp.log2(jnp.maximum(peak, 2.0**-100))) - 15.0
        out_ref[:, part * half : (part + 1) * half] = (
            value * power_of_two(-exponent)
        ).astype(out_ref.dtype)
        exponents = jnp.where(lane == part, exponent, exponents)
    out_ref[:, 3 * half :] = exponents.astype(out_ref.dtype)


def products_kernel(
    all_ref, kept_ref, gate_ref, up_ref, down_ref,
    send_ref, gate_sum_ref, up_sum_ref, down_sum_ref,
    hid_ref, dgate_ref, dup_ref, out_ref, rows_ref, sem,
):
    kept, hidden = hid_ref.shape
    half = hidden // 2
    width = gate_ref.shape[0]
    side = out_ref.shape[1] // 2
    block = all_ref.shape[0] // 16
    for index in range(16):
        chip, core = index // 2, index % 2
        lines = slice(index * block, (index + 1) * block)
        scale = power_of_two(all_ref[lines, 3 * half :].astype(F32))
        for part, ref in enumerate((hid_ref, dgate_ref, dup_ref)):
            ref[chip * block : (chip + 1) * block, core * half : (core + 1) * half] = (
                all_ref[lines, part * half : (part + 1) * half].astype(F32)
                * scale[:, part : part + 1]
            ).astype(BF16)
    out_ref[...] = jnp.zeros_like(out_ref)
    out_ref[:, 0:width] = mm(hid_ref[...], down_ref[...], NT).astype(BF16)
    out_ref[:, side : side + width] = (
        mm(dgate_ref[...], gate_ref[...], NT) + mm(dup_ref[...], up_ref[...], NT)
    ).astype(BF16)
    rows_ref[...] = mm(slot_matrix(rows_ref.shape[0], kept, True), out_ref[...]).astype(BF16)
    copy = pltpu.make_async_copy(rows_ref, send_ref, sem)
    copy.start()
    token_rows = kept_ref[:, 0:width]
    grad_rows = kept_ref[:, side : side + width]
    gate_sum_ref[...] = mm(token_rows, dgate_ref[...], TN).astype(BF16)
    up_sum_ref[...] = mm(token_rows, dup_ref[...], TN).astype(BF16)
    down_sum_ref[...] = mm(grad_rows, hid_ref[...], TN).astype(BF16)
    copy.wait()


def combine_kernel(back_ref, mark_ref, scale_ref, mixed_ref, token_grad_ref):
    tokens, width = mixed_ref.shape
    side = back_ref.shape[1] // 2
    for ref, marks, lo in ((mixed_ref, scale_ref, 0), (token_grad_ref, mark_ref, side)):
        parts = mm(marks[...], back_ref[:, lo : lo + width], TN).astype(BF16).astype(F32)
        ref[...] = (parts[0:tokens] + parts[tokens:]).astype(BF16)


def shards(tokens, expert_ids, route_weights, w_gate, w_up, w_down, grad_out):
    count, width = tokens.shape
    rep = lax.axis_size("rep")
    experts = lax.axis_size("node") * lax.axis_size("local")
    hidden = w_gate.shape[2]
    half = hidden // 2
    side = -(-width // 128) * 128
    node_hits = 2 * count // lax.axis_size("node")
    mean_count = 2 * node_hits // lax.axis_size("local")
    depth = min(mean_count + max(mean_count // 2, 1), node_hits)
    kept = experts * depth
    rows = experts * SLOTS
    lines = [list(range(c, rep, 2)) for c in range(2)]
    chips = rep // 2
    swap = [(i, i ^ 1) for i in range(rep)]
    core = (lax.axis_index("rep") % 2).astype(jnp.int32).reshape(1)
    gate_mat, up_mat, down_mat = w_gate[0], w_up[0], w_down[0].T

    routed = (expert_ids.T, route_weights.T, tokens, grad_out)
    send, mark, scale = call(
        route_kernel,
        [((rows, 2 * side), BF16), ((rows, 2 * count), BF16), ((rows, 2 * count), BF16)],
        *routed,
        far=(0, 1, 2),
        far_in=True,
        limit=60 * 1024 * 1024,
        scratch=[pltpu.VMEM(a.shape, a.dtype) for a in routed]
        + [pltpu.VMEM((rows, 2 * side), BF16)]
        + [pltpu.VMEM((rows, 2 * count), BF16)] * 2
        + [pltpu.SemaphoreType.DMA((7,))],
    )
    mine = lax.all_to_all(
        send.reshape(experts, SLOTS, 2 * side), ("node", "local"), 0, 0, tiled=True
    ).reshape(rows, 2 * side)
    packed = ((3 * width, half), BF16)
    own, give = call(
        pack_kernel, [packed, packed], core, gate_mat, up_mat, down_mat, scalars=1
    )
    other = lax.ppermute(give, "rep", swap)
    theirs = lax.ppermute(mine, "rep", swap)
    sums, kept_rows = call(
        sums_kernel,
        [((kept, 3 * half), BF16), ((kept, 2 * side), BF16)],
        mine, theirs, own, other,
        far=(1,),
        scratch=[pltpu.VMEM((kept, 2 * side), BF16), pltpu.SemaphoreType.DMA(())],
    )
    sums = lax.all_to_all(
        sums.reshape(chips, kept // chips, 3 * half),
        "rep", 0, 0, tiled=True, axis_index_groups=lines,
    )
    (piece,) = call(
        hidden_kernel, [((kept // chips, 3 * half + 128), BF16)], sums
    )
    piece = lax.optimization_barrier(piece.astype(jnp.float16))
    whole = lax.all_gather(piece, "rep", axis=0, tiled=True)
    whole = lax.optimization_barrier(whole).astype(BF16)
    matrix = pltpu.VMEM((kept, hidden), BF16)
    grads = ((width, hidden), BF16)
    send_back, gate_sum, up_sum, down_sum = call(
        products_kernel,
        [((rows, 2 * side), BF16), grads, grads, grads],
        whole, kept_rows, gate_mat, up_mat, down_mat,
        far=(0,),
        scratch=[
            matrix, matrix, matrix,
            pltpu.VMEM((kept, 2 * side), BF16),
            pltpu.VMEM((rows, 2 * side), BF16),
            pltpu.SemaphoreType.DMA(()),
        ],
    )
    back = lax.all_to_all(
        send_back.reshape(experts, SLOTS, 2 * side), ("node", "local"), 0, 0, tiled=True
    )
    mixed, token_grad = call(
        combine_kernel,
        [(tokens.shape, BF16), (tokens.shape, BF16)],
        back.reshape(rows, 2 * side), mark, scale,
    )
    return (mixed, token_grad, gate_sum[None], up_sum[None], down_sum.T[None])


def solution(mesh):
    return jax.shard_map(
        shards,
        mesh=mesh,
        in_specs=(
            P(("node", "local"), "rep"),
            P(("node", "local"), None),
            P(("node", "local"), None),
            P(("node", "local"), "rep", None),
            P(("node", "local"), "rep", None),
            P(("node", "local"), None, "rep"),
            P(("node", "local"), "rep"),
        ),
        out_specs=(
            P(("node", "local"), "rep"),
            P(("node", "local"), "rep"),
            P(("node", "local"), "rep", None),
            P(("node", "local"), "rep", None),
            P(("node", "local"), None, "rep"),
        ),
        check_vma=False,
    )
```

```python
import jax
import jax.numpy as jnp
from jax import lax
from jax.experimental import pallas as pl
from jax.experimental.pallas import tpu as pltpu
from jax.sharding import PartitionSpec as P

BF16 = jnp.bfloat16
F32 = jnp.float32
SLOTS = 8
LIMIT = 40 * 1024 * 1024

NN = (((1,), (0,)), ((), ()))
NT = (((1,), (1,)), ((), ()))
TN = (((0,), (0,)), ((), ()))


def mm(a, b, dims=NN):
    return lax.dot_general(a, b, dims, preferred_element_type=F32)


def call(kernel, outs, *args, scalars=0, far=(), far_in=False, scratch=(), limit=LIMIT):
    near = pl.BlockSpec(memory_space=pltpu.VMEM)
    away = pl.BlockSpec(memory_space=pl.ANY)
    specs = [pl.BlockSpec(memory_space=pltpu.SMEM)] * scalars
    specs += [away if far_in else near] * (len(args) - scalars)
    return pl.pallas_call(
        kernel,
        out_shape=[jax.ShapeDtypeStruct(shape, dtype) for shape, dtype in outs],
        in_specs=specs,
        out_specs=[away if i in far else near for i in range(len(outs))],
        scratch_shapes=list(scratch),
        compiler_params=pltpu.CompilerParams(vmem_limit_bytes=limit),
    )(*args)


def pack_kernel(core_ref, gate_ref, up_ref, down_ref, own_ref, send_ref):
    width, hidden = gate_ref.shape
    half = hidden // 2
    for ref, which in ((own_ref, core_ref[0]), (send_ref, 1 - core_ref[0])):
        start = pl.multiple_of(which * half, half)
        for part, mat_ref in enumerate((gate_ref, up_ref, down_ref)):
            ref[part * width : (part + 1) * width, :] = mat_ref[:, pl.ds(start, half)]


def route_kernel(
    ids_in, weight_in, token_in, grad_in, send_out, mark_out, scale_out,
    ids_ref, weight_ref, token_ref, grad_ref, send_ref, mark_ref, scale_ref, sems,
):
    pairs = (
        (ids_in, ids_ref), (weight_in, weight_ref), (token_in, token_ref), (grad_in, grad_ref),
        (mark_ref, mark_out), (scale_ref, scale_out), (send_ref, send_out),
    )
    copies = [pltpu.make_async_copy(*pair, sems.at[i]) for i, pair in enumerate(pairs)]
    for copy in copies[:4]:
        copy.start()
    copies[0].wait()
    copies[1].wait()
    picks, tokens = ids_ref.shape
    width = token_ref.shape[1]
    kept = mark_ref.shape[0]
    experts = send_ref.shape[0] // SLOTS
    row_i = lax.broadcasted_iota(jnp.int32, (tokens, tokens), 0)
    col_i = lax.broadcasted_iota(jnp.int32, (tokens, tokens), 1)
    earlier = (row_i < col_i).astype(F32)
    ids = ids_ref[...].astype(F32)
    weights = weight_ref[...].astype(F32)
    expert_i = lax.broadcasted_iota(jnp.int32, (experts, tokens), 0).astype(F32)
    row_all = lax.broadcasted_iota(jnp.int32, (kept, tokens), 0).astype(F32)
    before = jnp.zeros((experts, 1), F32)
    marks, scales = [], []
    for pick in range(picks):
        hit = (expert_i == ids[pick : pick + 1, :]).astype(F32)
        count = mm(hit, earlier) + before
        slot = jnp.sum(hit * count, axis=0, keepdims=True)
        before = before + jnp.sum(hit, axis=1, keepdims=True)
        found = row_all == slot * experts + ids[pick : pick + 1, :]
        marks.append(jnp.where(found, 1.0, 0.0))
        scales.append(jnp.where(found, weights[pick : pick + 1, :], 0.0))
    mark = jnp.concatenate([marks[0] + marks[1], marks[2] + marks[3]], axis=1).astype(BF16)
    scale = jnp.concatenate([scales[0] + scales[1], scales[2] + scales[3]], axis=1).astype(BF16)
    mark_ref[...] = mark
    scale_ref[...] = scale
    copies[4].start()
    copies[5].start()
    copies[2].wait()
    copies[3].wait()
    twice = lambda ref: jnp.concatenate([ref[...], ref[...]], axis=0)
    pack_rows(
        mm(mark, twice(token_ref)).astype(BF16),
        mm(scale, twice(grad_ref)).astype(BF16),
        send_ref,
    )
    copies[6].start()
    for copy in copies[4:]:
        copy.wait()


def one_hot(rows, places, turned):
    shape = (rows, places.shape[1]) if turned else (places.shape[0], rows)
    return (lax.broadcasted_iota(jnp.int32, shape, 0 if turned else 1) == places).astype(BF16)


def slot_matrix(rows, kept, turned):
    sources = rows // SLOTS
    index = lax.broadcasted_iota(jnp.int32, (1, kept) if turned else (kept, 1), int(turned))
    return one_hot(rows, lax.rem(index, sources) * SLOTS + index // sources, turned)


def spare_matrix(rows, turned):
    sources = rows // SLOTS
    shape = (1, sources) if turned else (sources, 1)
    index = lax.broadcasted_iota(jnp.int32, shape, int(turned))
    return one_hot(rows, index * SLOTS + SLOTS - 2, turned)


def pack_rows(first, second, sent_ref):
    rows, lanes = sent_ref.shape
    kept, width = first.shape
    sources = rows // SLOTS
    cut = lanes - width
    wide = jnp.concatenate([first, second[:, :cut]], axis=1)
    spare = jnp.concatenate(
        [second[i : i + sources, cut:] for i in range(0, kept, sources)], axis=1
    )
    sent_ref[...] = (
        mm(slot_matrix(rows, kept, True), wide) + mm(spare_matrix(rows, True), spare)
    ).astype(BF16)


def unpack_rows(sent, kept, width):
    rows, lanes = sent.shape
    sources = rows // SLOTS
    rest = 2 * width - lanes
    wide = mm(slot_matrix(rows, kept, False), sent).astype(BF16)
    spare = mm(spare_matrix(rows, False), sent).astype(BF16)
    tail = jnp.concatenate(
        [spare[:, i * rest : (i + 1) * rest] for i in range(kept // sources)], axis=0
    )
    return wide[:, :width], jnp.concatenate([wide[:, width:], tail], axis=1)


def sums_kernel(
    mine_ref, theirs_ref, own_ref, other_ref, sum_ref, kept_out, kept_ref, sem
):
    kept = sum_ref.shape[0]
    half = own_ref.shape[1]
    width = own_ref.shape[0] // 3
    side = kept_ref.shape[1] // 2
    mine = unpack_rows(mine_ref[...], kept, width)
    kept_ref[...] = jnp.zeros_like(kept_ref)
    kept_ref[:, 0:width] = mine[0]
    kept_ref[:, side : side + width] = mine[1]
    copy = pltpu.make_async_copy(kept_ref, kept_out, sem)
    copy.start()
    theirs = unpack_rows(theirs_ref[...], kept, width)
    for part, which in enumerate((0, 0, 1)):
        block = slice(part * width, (part + 1) * width)
        sum_ref[:, part * half : (part + 1) * half] = (
            mm(mine[which], own_ref[block, :]) + mm(theirs[which], other_ref[block, :])
        ).astype(BF16)
    copy.wait()


def power_of_two(exponent):
    left = jnp.abs(exponent)
    result = jnp.ones_like(exponent)
    for bit in (64, 32, 16, 8, 4, 2, 1):
        taken = left >= bit
        step = jnp.where(exponent >= 0, 2.0**bit, 2.0**-bit)
        result = jnp.where(taken, result * step, result)
        left = jnp.where(taken, left - bit, left)
    return result


def hidden_kernel(sum_ref, out_ref):
    half = sum_ref.shape[2] // 3
    total = lambda part: jnp.sum(
        sum_ref[:, :, part * half : (part + 1) * half].astype(F32), axis=0
    )
    gate, up, back = total(0), total(1), total(2)
    sig = jax.nn.sigmoid(gate)
    values = (
        gate * sig * up,
        back * up * (sig * (1.0 + gate * (1.0 - sig))),
        back * (gate * sig),
    )
    lane = lax.broadcasted_iota(jnp.int32, (gate.shape[0], 128), 1)
    exponents = jnp.zeros(lane.shape, F32)
    for part, value in enumerate(values):
        value = value.astype(BF16).astype(F32)
        peak = jnp.max(jnp.abs(value), axis=1, keepdims=True)
        exponent = jnp.ceil(jnp.log2(jnp.maximum(peak, 2.0**-100))) - 15.0
        out_ref[:, part * half : (part + 1) * half] = (
            value * power_of_two(-exponent)
        ).astype(out_ref.dtype)
        exponents = jnp.where(lane == part, exponent, exponents)
    out_ref[:, 3 * half :] = exponents.astype(out_ref.dtype)


def products_kernel(
    all_ref, kept_ref, gate_ref, up_ref, down_ref,
    send_ref, gate_sum_ref, up_sum_ref, down_sum_ref,
    hid_ref, dgate_ref, dup_ref, rows_ref, sem,
):
    kept, hidden = hid_ref.shape
    half = hidden // 2
    width = gate_ref.shape[0]
    side = kept_ref.shape[1] // 2
    block = all_ref.shape[0] // 16
    for index in range(16):
        chip, core = index // 2, index % 2
        lines = slice(index * block, (index + 1) * block)
        scale = power_of_two(all_ref[lines, 3 * half :].astype(F32))
        for part, ref in enumerate((hid_ref, dgate_ref, dup_ref)):
            ref[chip * block : (chip + 1) * block, core * half : (core + 1) * half] = (
                all_ref[lines, part * half : (part + 1) * half].astype(F32)
                * scale[:, part : part + 1]
            ).astype(BF16)
    out_rows = mm(hid_ref[...], down_ref[...], NT).astype(BF16)
    back_rows = (
        mm(dgate_ref[...], gate_ref[...], NT) + mm(dup_ref[...], up_ref[...], NT)
    ).astype(BF16)
    pack_rows(out_rows, back_rows, rows_ref)
    copy = pltpu.make_async_copy(rows_ref, send_ref, sem)
    copy.start()
    token_rows = kept_ref[:, 0:width]
    grad_rows = kept_ref[:, side : side + width]
    gate_sum_ref[...] = mm(token_rows, dgate_ref[...], TN).astype(BF16)
    up_sum_ref[...] = mm(token_rows, dup_ref[...], TN).astype(BF16)
    down_sum_ref[...] = mm(grad_rows, hid_ref[...], TN).astype(BF16)
    copy.wait()


def combine_kernel(back_ref, mark_ref, scale_ref, mixed_ref, token_grad_ref):
    tokens, width = mixed_ref.shape
    back = unpack_rows(back_ref[...], mark_ref.shape[0], width)
    for ref, marks, values in zip((mixed_ref, token_grad_ref), (scale_ref, mark_ref), back):
        parts = mm(marks[...], values, TN).astype(BF16).astype(F32)
        ref[...] = (parts[0:tokens] + parts[tokens:]).astype(BF16)


def shards(tokens, expert_ids, route_weights, w_gate, w_up, w_down, grad_out):
    count, width = tokens.shape
    rep = lax.axis_size("rep")
    experts = lax.axis_size("node") * lax.axis_size("local")
    hidden = w_gate.shape[2]
    half = hidden // 2
    side = -(-width // 128) * 128
    node_hits = 2 * count // lax.axis_size("node")
    mean_count = 2 * node_hits // lax.axis_size("local")
    depth = min(mean_count + max(mean_count // 2, 1), node_hits)
    kept = experts * depth
    rows = experts * SLOTS
    lanes = 2 * width * depth // (depth + 1)
    lines = [list(range(c, rep, 2)) for c in range(2)]
    chips = rep // 2
    swap = [(i, i ^ 1) for i in range(rep)]
    core = (lax.axis_index("rep") % 2).astype(jnp.int32).reshape(1)
    gate_mat, up_mat, down_mat = w_gate[0], w_up[0], w_down[0].T

    routed = (expert_ids.T, route_weights.T, tokens, grad_out)
    send, mark, scale = call(
        route_kernel,
        [((rows, lanes), BF16), ((kept, 2 * count), BF16), ((kept, 2 * count), BF16)],
        *routed,
        far=(0, 1, 2),
        far_in=True,
        limit=60 * 1024 * 1024,
        scratch=[pltpu.VMEM(a.shape, a.dtype) for a in routed]
        + [pltpu.VMEM((rows, lanes), BF16)]
        + [pltpu.VMEM((kept, 2 * count), BF16)] * 2
        + [pltpu.SemaphoreType.DMA((7,))],
    )
    mine = lax.all_to_all(
        send.reshape(experts, SLOTS, lanes), ("node", "local"), 0, 0, tiled=True
    ).reshape(rows, lanes)
    packed = ((3 * width, half), BF16)
    own, give = call(
        pack_kernel, [packed, packed], core, gate_mat, up_mat, down_mat, scalars=1
    )
    other = lax.ppermute(give, "rep", swap)
    theirs = lax.ppermute(mine, "rep", swap)
    sums, kept_rows = call(
        sums_kernel,
        [((kept, 3 * half), BF16), ((kept, 2 * side), BF16)],
        mine, theirs, own, other,
        far=(1,),
        scratch=[pltpu.VMEM((kept, 2 * side), BF16), pltpu.SemaphoreType.DMA(())],
    )
    sums = lax.all_to_all(
        sums.reshape(chips, kept // chips, 3 * half),
        "rep", 0, 0, tiled=True, axis_index_groups=lines,
    )
    (piece,) = call(
        hidden_kernel, [((kept // chips, 3 * half + 128), BF16)], sums
    )
    piece = lax.optimization_barrier(piece.astype(jnp.float16))
    whole = lax.all_gather(piece, "rep", axis=0, tiled=True)
    whole = lax.optimization_barrier(whole).astype(BF16)
    matrix = pltpu.VMEM((kept, hidden), BF16)
    grads = ((width, hidden), BF16)
    send_back, gate_sum, up_sum, down_sum = call(
        products_kernel,
        [((rows, lanes), BF16), grads, grads, grads],
        whole, kept_rows, gate_mat, up_mat, down_mat,
        far=(0,),
        scratch=[
            matrix, matrix, matrix,
            pltpu.VMEM((rows, lanes), BF16),
            pltpu.SemaphoreType.DMA(()),
        ],
    )
    back = lax.all_to_all(
        send_back.reshape(experts, SLOTS, lanes), ("node", "local"), 0, 0, tiled=True
    )
    mixed, token_grad = call(
        combine_kernel,
        [(tokens.shape, BF16), (tokens.shape, BF16)],
        back.reshape(rows, lanes), mark, scale,
    )
    return (mixed, token_grad, gate_sum[None], up_sum[None], down_sum.T[None])


def solution(mesh):
    return jax.shard_map(
        shards,
        mesh=mesh,
        in_specs=(
            P(("node", "local"), "rep"),
            P(("node", "local"), None),
            P(("node", "local"), None),
            P(("node", "local"), "rep", None),
            P(("node", "local"), "rep", None),
            P(("node", "local"), None, "rep"),
            P(("node", "local"), "rep"),
        ),
        out_specs=(
            P(("node", "local"), "rep"),
            P(("node", "local"), "rep"),
            P(("node", "local"), "rep", None),
            P(("node", "local"), "rep", None),
            P(("node", "local"), None, "rep"),
        ),
        check_vma=False,
    )
```

```python
import jax
import jax.numpy as jnp
from jax import lax
from jax.experimental import pallas as pl
from jax.experimental.pallas import tpu as pltpu
from jax.sharding import PartitionSpec as P

BF16 = jnp.bfloat16
F32 = jnp.float32
SLOTS = 8
LIMIT = 40 * 1024 * 1024

NN = (((1,), (0,)), ((), ()))
NT = (((1,), (1,)), ((), ()))
TN = (((0,), (0,)), ((), ()))


def mm(a, b, dims=NN):
    return lax.dot_general(a, b, dims, preferred_element_type=F32)


def call(kernel, outs, *args, scalars=0, far=(), far_in=(), scratch=(), limit=LIMIT):
    near = pl.BlockSpec(memory_space=pltpu.VMEM)
    away = pl.BlockSpec(memory_space=pl.ANY)
    specs = [pl.BlockSpec(memory_space=pltpu.SMEM)] * scalars
    specs += [away if i in far_in else near for i in range(scalars, len(args))]
    return pl.pallas_call(
        kernel,
        out_shape=[jax.ShapeDtypeStruct(shape, dtype) for shape, dtype in outs],
        in_specs=specs,
        out_specs=[away if i in far else near for i in range(len(outs))],
        scratch_shapes=list(scratch),
        compiler_params=pltpu.CompilerParams(vmem_limit_bytes=limit),
    )(*args)


def pack_kernel(core_ref, gate_ref, up_ref, down_ref, own_ref, send_ref):
    width, hidden = gate_ref.shape
    half = hidden // 2
    for ref, which in ((own_ref, core_ref[0]), (send_ref, 1 - core_ref[0])):
        start = pl.multiple_of(which * half, half)
        for part, mat_ref in enumerate((gate_ref, up_ref, down_ref)):
            ref[part * width : (part + 1) * width, :] = mat_ref[:, pl.ds(start, half)]


def route_kernel(
    ids_in, weight_in, token_in, grad_in, send_out, mark_out, scale_out,
    ids_ref, weight_ref, token_ref, grad_ref, send_ref, mark_ref, scale_ref, sems,
):
    pairs = (
        (ids_in, ids_ref), (weight_in, weight_ref), (token_in, token_ref), (grad_in, grad_ref),
        (mark_ref, mark_out), (scale_ref, scale_out),
    )
    copies = [pltpu.make_async_copy(*pair, sems.at[i]) for i, pair in enumerate(pairs)]

    def leave(lines):
        copies.append(
            pltpu.make_async_copy(
                send_ref.at[lines, :], send_out.at[lines, :], sems.at[len(copies)]
            )
        )
        copies[-1].start()

    for copy in copies[:4]:
        copy.start()
    copies[0].wait()
    copies[1].wait()
    picks, tokens = ids_ref.shape
    width = token_ref.shape[1]
    kept = mark_ref.shape[0]
    experts = send_ref.shape[0] // SLOTS
    row_i = lax.broadcasted_iota(jnp.int32, (tokens, tokens), 0)
    col_i = lax.broadcasted_iota(jnp.int32, (tokens, tokens), 1)
    earlier = (row_i < col_i).astype(F32)
    ids = ids_ref[...].astype(F32)
    weights = weight_ref[...].astype(F32)
    expert_i = lax.broadcasted_iota(jnp.int32, (experts, tokens), 0).astype(F32)
    row_all = lax.broadcasted_iota(jnp.int32, (kept, tokens), 0).astype(F32)
    hits = [(expert_i == ids[pick : pick + 1, :]).astype(F32) for pick in range(picks)]
    counts = mm(jnp.concatenate(hits, axis=0).astype(BF16), earlier.astype(BF16))
    before = jnp.zeros((experts, 1), F32)
    marks, scales = [], []
    for pick, hit in enumerate(hits):
        count = counts[pick * experts : (pick + 1) * experts] + before
        slot = jnp.sum(hit * count, axis=0, keepdims=True)
        before = before + jnp.sum(hit, axis=1, keepdims=True)
        found = row_all == slot * experts + ids[pick : pick + 1, :]
        marks.append(jnp.where(found, 1.0, 0.0))
        scales.append(jnp.where(found, weights[pick : pick + 1, :], 0.0))
    mark = jnp.concatenate([marks[0] + marks[1], marks[2] + marks[3]], axis=1).astype(BF16)
    scale = jnp.concatenate([scales[0] + scales[1], scales[2] + scales[3]], axis=1).astype(BF16)
    mark_ref[...] = mark
    scale_ref[...] = scale
    copies[4].start()
    copies[5].start()
    copies[2].wait()
    copies[3].wait()
    twice = lambda ref: jnp.concatenate([ref[...], ref[...]], axis=0)
    pack_rows(
        mm(mark, twice(token_ref)).astype(BF16),
        mm(scale, twice(grad_ref)).astype(BF16),
        send_ref,
        4,
        leave,
    )
    for copy in copies[4:]:
        copy.wait()


def one_hot(rows, places, turned):
    shape = (rows, places.shape[1]) if turned else (places.shape[0], rows)
    return (lax.broadcasted_iota(jnp.int32, shape, 0 if turned else 1) == places).astype(BF16)


def slot_places(rows, kept, shape=None):
    sources = rows // SLOTS
    shape = shape or (1, kept)
    index = lax.broadcasted_iota(jnp.int32, shape, 0 if shape[1] == 1 else 1)
    return lax.rem(index, sources) * SLOTS + index // sources


def spare_places(rows, shape=None):
    shape = shape or (1, rows // SLOTS)
    index = lax.broadcasted_iota(jnp.int32, shape, 0 if shape[1] == 1 else 1)
    return index * SLOTS + SLOTS - 2


def pack_rows(first, second, sent_ref, blocks, leave):
    rows, lanes = sent_ref.shape
    kept, width = first.shape
    sources = rows // SLOTS
    cut = lanes - width
    wide = jnp.concatenate([first, second[:, :cut]], axis=1)
    spare = jnp.concatenate(
        [second[i : i + sources, cut:] for i in range(0, kept, sources)], axis=1
    )
    both = jnp.concatenate([wide, spare], axis=0)
    places = jnp.concatenate([slot_places(rows, kept), spare_places(rows)], axis=1)
    size = rows // blocks
    for block in range(blocks):
        lines = slice(block * size, (block + 1) * size)
        sent_ref[lines, :] = mm(
            one_hot(size, places - block * size, True), both
        ).astype(BF16)
        leave(lines)


def unpack_tail(sent, rest):
    rows, lanes = sent.shape
    places = spare_places(rows, (rows // SLOTS, 1))
    spare = mm(one_hot(rows, places, False), sent).astype(BF16)
    return jnp.concatenate([spare[:, i : i + rest] for i in range(0, lanes, rest)], axis=0)


def unpack_rows(sent, kept, width):
    rows, lanes = sent.shape
    wide = mm(one_hot(rows, slot_places(rows, kept, (kept, 1)), False), sent).astype(BF16)
    tail = unpack_tail(sent, 2 * width - lanes)
    return wide[:, :width], jnp.concatenate([wide[:, width:], tail], axis=1)


def part_sums(rows, half_ref):
    width = half_ref.shape[0] // 3
    for part, which in enumerate((0, 0, 1)):
        yield part, mm(rows[which], half_ref[part * width : (part + 1) * width, :])


def own_kernel(mine_ref, own_ref, sum_ref, kept_out, kept_ref, sem):
    kept, wide = kept_ref.shape
    half = own_ref.shape[1]
    width = own_ref.shape[0] // 3
    mine = unpack_rows(mine_ref[...], kept, width)
    kept_ref[...] = jnp.zeros_like(kept_ref)
    kept_ref[:, 0:width] = mine[0]
    kept_ref[:, wide // 2 : wide // 2 + width] = mine[1]
    copy = pltpu.make_async_copy(kept_ref, kept_out, sem)
    copy.start()
    for part, value in part_sums(mine, own_ref):
        sum_ref[:, part * half : (part + 1) * half] = value
    copy.wait()


def sums_kernel(theirs_ref, other_ref, part_ref, sum_ref):
    half = other_ref.shape[1]
    theirs = unpack_rows(theirs_ref[...], sum_ref.shape[0], other_ref.shape[0] // 3)
    for part, value in part_sums(theirs, other_ref):
        columns = slice(part * half, (part + 1) * half)
        sum_ref[:, columns] = (part_ref[:, columns] + value).astype(BF16)


def power_of_two(exponent):
    left = jnp.abs(exponent)
    result = jnp.ones_like(exponent)
    for bit in (64, 32, 16, 8, 4, 2, 1):
        taken = left >= bit
        step = jnp.where(exponent >= 0, 2.0**bit, 2.0**-bit)
        result = jnp.where(taken, result * step, result)
        left = jnp.where(taken, left - bit, left)
    return result


def hidden_kernel(sum_ref, out_ref):
    half = sum_ref.shape[2] // 3
    total = lambda part: jnp.sum(
        sum_ref[:, :, part * half : (part + 1) * half].astype(F32), axis=0
    )
    gate, up, back = total(0), total(1), total(2)
    sig = jax.nn.sigmoid(gate)
    values = (
        gate * sig * up,
        back * up * (sig * (1.0 + gate * (1.0 - sig))),
        back * (gate * sig),
    )
    lane = lax.broadcasted_iota(jnp.int32, (gate.shape[0], 128), 1)
    exponents = jnp.zeros(lane.shape, F32)
    for part, value in enumerate(values):
        value = value.astype(BF16).astype(F32)
        peak = jnp.max(jnp.abs(value), axis=1, keepdims=True)
        exponent = jnp.ceil(jnp.log2(jnp.maximum(peak, 2.0**-100))) - 15.0
        out_ref[:, part * half : (part + 1) * half] = (
            value * power_of_two(-exponent)
        ).astype(out_ref.dtype)
        exponents = jnp.where(lane == part, exponent, exponents)
    out_ref[:, 3 * half :] = exponents.astype(out_ref.dtype)


def products_kernel(
    all_ref, kept_ref, gate_ref, up_ref, down_ref,
    send_out, gate_out, up_out, down_out,
    hid_ref, dgate_ref, dup_ref, rows_ref, gate_sum_ref, up_sum_ref, down_sum_ref,
    sems,
):
    kept, hidden = hid_ref.shape
    half = hidden // 2
    width = gate_ref.shape[0]
    side = kept_ref.shape[1] // 2
    block = all_ref.shape[0] // 16
    for index in range(16):
        chip, core = index // 2, index % 2
        lines = slice(index * block, (index + 1) * block)
        scale = power_of_two(all_ref[lines, 3 * half :].astype(F32))
        for part, ref in enumerate((hid_ref, dgate_ref, dup_ref)):
            ref[chip * block : (chip + 1) * block, core * half : (core + 1) * half] = (
                all_ref[lines, part * half : (part + 1) * half].astype(F32)
                * scale[:, part : part + 1]
            ).astype(BF16)
    token_rows = kept_ref[:, 0:width]
    grad_rows = kept_ref[:, side : side + width]
    copies = []

    def leave(ref, out):
        copies.append(pltpu.make_async_copy(ref, out, sems.at[len(copies)]))
        copies[-1].start()

    def leave_rows(lines):
        leave(rows_ref.at[lines, :], send_out.at[lines, :])

    for ref, out, rows, values_ref in (
        (gate_sum_ref, gate_out, token_rows, dgate_ref),
        (up_sum_ref, up_out, token_rows, dup_ref),
        (down_sum_ref, down_out, grad_rows, hid_ref),
    ):
        ref[...] = mm(rows, values_ref[...], TN).astype(BF16)
        leave(ref, out)
    out_rows = mm(hid_ref[...], down_ref[...], NT).astype(BF16)
    back_rows = (
        mm(dgate_ref[...], gate_ref[...], NT) + mm(dup_ref[...], up_ref[...], NT)
    ).astype(BF16)
    pack_rows(out_rows, back_rows, rows_ref, 4, leave_rows)
    for copy in copies:
        copy.wait()


def combine_kernel(back_ref, mark_ref, scale_ref, mixed_ref, token_grad_ref):
    tokens, width = mixed_ref.shape
    back = unpack_rows(back_ref[...], mark_ref.shape[0], width)
    for ref, marks, values in zip((mixed_ref, token_grad_ref), (scale_ref, mark_ref), back):
        parts = mm(marks[...], values, TN).astype(BF16).astype(F32)
        ref[...] = (parts[0:tokens] + parts[tokens:]).astype(BF16)


def shards(tokens, expert_ids, route_weights, w_gate, w_up, w_down, grad_out):
    count, width = tokens.shape
    rep = lax.axis_size("rep")
    experts = lax.axis_size("node") * lax.axis_size("local")
    hidden = w_gate.shape[2]
    half = hidden // 2
    side = -(-width // 128) * 128
    node_hits = 2 * count // lax.axis_size("node")
    mean_count = 2 * node_hits // lax.axis_size("local")
    depth = min(mean_count + max(mean_count // 2, 1), node_hits)
    kept = experts * depth
    rows = experts * SLOTS
    lanes = 2 * width * depth // (depth + 1)
    lines = [list(range(c, rep, 2)) for c in range(2)]
    chips = rep // 2
    swap = [(i, i ^ 1) for i in range(rep)]
    core = (lax.axis_index("rep") % 2).astype(jnp.int32).reshape(1)
    gate_mat, up_mat, down_mat = w_gate[0], w_up[0], w_down[0].T

    routed = (expert_ids.T, route_weights.T, tokens, grad_out)
    send, mark, scale = call(
        route_kernel,
        [((rows, lanes), BF16), ((kept, 2 * count), BF16), ((kept, 2 * count), BF16)],
        *routed,
        far=(0, 1, 2),
        far_in=(0, 1, 2, 3),
        limit=60 * 1024 * 1024,
        scratch=[pltpu.VMEM(a.shape, a.dtype) for a in routed]
        + [pltpu.VMEM((rows, lanes), BF16)]
        + [pltpu.VMEM((kept, 2 * count), BF16)] * 2
        + [pltpu.SemaphoreType.DMA((10,))],
    )
    mine = lax.all_to_all(
        send.reshape(experts, SLOTS, lanes), ("node", "local"), 0, 0, tiled=True
    ).reshape(rows, lanes)
    packed = ((3 * width, half), BF16)
    own, give = call(
        pack_kernel, [packed, packed], core, gate_mat, up_mat, down_mat, scalars=1
    )
    other = lax.ppermute(give, "rep", swap)
    theirs = lax.ppermute(mine, "rep", swap)
    sums, kept_rows = call(
        own_kernel,
        [((kept, 3 * half), F32), ((kept, 2 * side), BF16)],
        mine, own,
        far=(1,),
        scratch=[pltpu.VMEM((kept, 2 * side), BF16), pltpu.SemaphoreType.DMA(())],
    )
    (sums,) = call(sums_kernel, [((kept, 3 * half), BF16)], theirs, other, sums)
    sums = lax.all_to_all(
        sums.reshape(chips, kept // chips, 3 * half),
        "rep", 0, 0, tiled=True, axis_index_groups=lines,
    )
    (piece,) = call(
        hidden_kernel, [((kept // chips, 3 * half + 128), BF16)], sums
    )
    piece = lax.optimization_barrier(piece.astype(jnp.float16))
    whole = lax.all_gather(piece, "rep", axis=0, tiled=True)
    whole = lax.optimization_barrier(whole).astype(BF16)
    matrix = pltpu.VMEM((kept, hidden), BF16)
    grads = ((width, hidden), BF16)
    send_back, gate_sum, up_sum, down_sum = call(
        products_kernel,
        [((rows, lanes), BF16), grads, grads, grads],
        whole, kept_rows, gate_mat, up_mat, down_mat,
        far=(0, 1, 2, 3),
        scratch=[
            matrix, matrix, matrix,
            pltpu.VMEM((rows, lanes), BF16),
            *[pltpu.VMEM(*grads)] * 3,
            pltpu.SemaphoreType.DMA((7,)),
        ],
    )
    back = lax.all_to_all(
        send_back.reshape(experts, SLOTS, lanes), ("node", "local"), 0, 0, tiled=True
    )
    mixed, token_grad = call(
        combine_kernel,
        [(tokens.shape, BF16), (tokens.shape, BF16)],
        back.reshape(rows, lanes), mark, scale,
    )
    return (mixed, token_grad, gate_sum[None], up_sum[None], down_sum.T[None])


def solution(mesh):
    return jax.shard_map(
        shards,
        mesh=mesh,
        in_specs=(
            P(("node", "local"), "rep"),
            P(("node", "local"), None),
            P(("node", "local"), None),
            P(("node", "local"), "rep", None),
            P(("node", "local"), "rep", None),
            P(("node", "local"), None, "rep"),
            P(("node", "local"), "rep"),
        ),
        out_specs=(
            P(("node", "local"), "rep"),
            P(("node", "local"), "rep"),
            P(("node", "local"), "rep", None),
            P(("node", "local"), "rep", None),
            P(("node", "local"), None, "rep"),
        ),
        check_vma=False,
    )
```

```python
import jax
import jax.numpy as jnp
from jax import lax
from jax.experimental import pallas as pl
from jax.experimental.pallas import tpu as pltpu
from jax.sharding import PartitionSpec as P

BF16 = jnp.bfloat16
F32 = jnp.float32
SLOTS = 8
LIMIT = 40 * 1024 * 1024

NN = (((1,), (0,)), ((), ()))
NT = (((1,), (1,)), ((), ()))
TN = (((0,), (0,)), ((), ()))


def mm(a, b, dims=NN):
    return lax.dot_general(a, b, dims, preferred_element_type=F32)


def call(kernel, outs, *args, scalars=0, far=(), far_in=(), scratch=(), limit=LIMIT):
    near = pl.BlockSpec(memory_space=pltpu.VMEM)
    away = pl.BlockSpec(memory_space=pl.ANY)
    specs = [pl.BlockSpec(memory_space=pltpu.SMEM)] * scalars
    specs += [away if i in far_in else near for i in range(scalars, len(args))]
    return pl.pallas_call(
        kernel,
        out_shape=[jax.ShapeDtypeStruct(shape, dtype) for shape, dtype in outs],
        in_specs=specs,
        out_specs=[away if i in far else near for i in range(len(outs))],
        scratch_shapes=list(scratch),
        compiler_params=pltpu.CompilerParams(vmem_limit_bytes=limit),
    )(*args)


def pack_kernel(
    core_ref, gate_ref, up_ref, down_ref, mark_ref, scale_ref,
    own_ref, send_ref, mark_out, scale_out, tail_out,
):
    width, hidden = gate_ref.shape
    half = hidden // 2
    for ref, which in ((own_ref, core_ref[0]), (send_ref, 1 - core_ref[0])):
        start = pl.multiple_of(which * half, half)
        for part, mat_ref in enumerate((gate_ref, up_ref, down_ref)):
            ref[part * width : (part + 1) * width, :] = mat_ref[:, pl.ds(start, half)]
    kept, rows = mark_ref.shape[0], mark_out.shape[1]
    pack = one_hot(rows, slot_places(rows, kept, (kept, 1)), False)
    mark_out[...] = mm(mark_ref[...], pack, TN).astype(BF16)
    scale_out[...] = mm(scale_ref[...], pack, TN).astype(BF16)
    tail_out[...] = mark_ref[...].T


def route_kernel(
    ids_in, weight_in, token_in, grad_in, send_out, mark_out, scale_out,
    ids_ref, weight_ref, token_ref, grad_ref, send_ref, mark_ref, scale_ref, sems,
):
    pairs = (
        (ids_in, ids_ref), (weight_in, weight_ref), (token_in, token_ref), (grad_in, grad_ref),
        (mark_ref, mark_out), (scale_ref, scale_out),
    )
    copies = [pltpu.make_async_copy(*pair, sems.at[i]) for i, pair in enumerate(pairs)]

    def leave(lines):
        copies.append(
            pltpu.make_async_copy(
                send_ref.at[lines, :], send_out.at[lines, :], sems.at[len(copies)]
            )
        )
        copies[-1].start()

    for copy in copies[:4]:
        copy.start()
    copies[0].wait()
    copies[1].wait()
    picks, tokens = ids_ref.shape
    width = token_ref.shape[1]
    kept = mark_ref.shape[0]
    experts = send_ref.shape[0] // SLOTS
    row_i = lax.broadcasted_iota(jnp.int32, (tokens, tokens), 0)
    col_i = lax.broadcasted_iota(jnp.int32, (tokens, tokens), 1)
    earlier = (row_i < col_i).astype(F32)
    ids = ids_ref[...].astype(F32)
    weights = weight_ref[...].astype(F32)
    expert_i = lax.broadcasted_iota(jnp.int32, (experts, tokens), 0).astype(F32)
    row_all = lax.broadcasted_iota(jnp.int32, (kept, tokens), 0).astype(F32)
    hits = [(expert_i == ids[pick : pick + 1, :]).astype(F32) for pick in range(picks)]
    counts = mm(jnp.concatenate(hits, axis=0).astype(BF16), earlier.astype(BF16))
    before = jnp.zeros((experts, 1), F32)
    marks, scales = [], []
    for pick, hit in enumerate(hits):
        count = counts[pick * experts : (pick + 1) * experts] + before
        slot = jnp.sum(hit * count, axis=0, keepdims=True)
        before = before + jnp.sum(hit, axis=1, keepdims=True)
        found = row_all == slot * experts + ids[pick : pick + 1, :]
        marks.append(jnp.where(found, 1.0, 0.0))
        scales.append(jnp.where(found, weights[pick : pick + 1, :], 0.0))
    mark = jnp.concatenate([marks[0] + marks[1], marks[2] + marks[3]], axis=1).astype(BF16)
    scale = jnp.concatenate([scales[0] + scales[1], scales[2] + scales[3]], axis=1).astype(BF16)
    mark_ref[...] = mark
    scale_ref[...] = scale
    copies[4].start()
    copies[5].start()
    copies[2].wait()
    copies[3].wait()
    twice = lambda ref: jnp.concatenate([ref[...], ref[...]], axis=0)
    pack_rows(
        mm(mark, twice(token_ref)).astype(BF16),
        mm(scale, twice(grad_ref)).astype(BF16),
        send_ref,
        4,
        leave,
    )
    for copy in copies[4:]:
        copy.wait()


def one_hot(rows, places, turned):
    shape = (rows, places.shape[1]) if turned else (places.shape[0], rows)
    return (lax.broadcasted_iota(jnp.int32, shape, 0 if turned else 1) == places).astype(BF16)


def slot_places(rows, kept, shape=None):
    sources = rows // SLOTS
    shape = shape or (1, kept)
    index = lax.broadcasted_iota(jnp.int32, shape, 0 if shape[1] == 1 else 1)
    return lax.rem(index, sources) * SLOTS + index // sources


def spare_places(rows, shape=None):
    shape = shape or (1, rows // SLOTS)
    index = lax.broadcasted_iota(jnp.int32, shape, 0 if shape[1] == 1 else 1)
    return index * SLOTS + SLOTS - 2


def pack_rows(first, second, sent_ref, blocks, leave):
    rows, lanes = sent_ref.shape
    kept, width = first.shape
    sources = rows // SLOTS
    cut = lanes - width
    wide = jnp.concatenate([first, second[:, :cut]], axis=1)
    spare = jnp.concatenate(
        [second[i : i + sources, cut:] for i in range(0, kept, sources)], axis=1
    )
    both = jnp.concatenate([wide, spare], axis=0)
    places = jnp.concatenate([slot_places(rows, kept), spare_places(rows)], axis=1)
    size = rows // blocks
    for block in range(blocks):
        lines = slice(block * size, (block + 1) * size)
        sent_ref[lines, :] = mm(
            one_hot(size, places - block * size, True), both
        ).astype(BF16)
        leave(lines)


def unpack_tail(sent, rest):
    rows, lanes = sent.shape
    places = spare_places(rows, (rows // SLOTS, 1))
    spare = mm(one_hot(rows, places, False), sent).astype(BF16)
    return jnp.concatenate([spare[:, i : i + rest] for i in range(0, lanes, rest)], axis=0)


def unpack_rows(sent, kept, width):
    rows, lanes = sent.shape
    wide = mm(one_hot(rows, slot_places(rows, kept, (kept, 1)), False), sent).astype(BF16)
    tail = unpack_tail(sent, 2 * width - lanes)
    return wide[:, :width], jnp.concatenate([wide[:, width:], tail], axis=1)


def part_sums(rows, half_ref):
    width = half_ref.shape[0] // 3
    for part, which in enumerate((0, 0, 1)):
        yield part, mm(rows[which], half_ref[part * width : (part + 1) * width, :])


def own_kernel(mine_ref, own_ref, sum_ref, kept_out, kept_ref, sem):
    kept, wide = kept_ref.shape
    half = own_ref.shape[1]
    width = own_ref.shape[0] // 3
    mine = unpack_rows(mine_ref[...], kept, width)
    kept_ref[...] = jnp.zeros_like(kept_ref)
    kept_ref[:, 0:width] = mine[0]
    kept_ref[:, wide // 2 : wide // 2 + width] = mine[1]
    copy = pltpu.make_async_copy(kept_ref, kept_out, sem)
    copy.start()
    for part, value in part_sums(mine, own_ref):
        sum_ref[:, part * half : (part + 1) * half] = value
    copy.wait()


def sums_kernel(theirs_ref, other_ref, part_ref, sum_ref):
    half = other_ref.shape[1]
    theirs = unpack_rows(theirs_ref[...], sum_ref.shape[0], other_ref.shape[0] // 3)
    for part, value in part_sums(theirs, other_ref):
        columns = slice(part * half, (part + 1) * half)
        sum_ref[:, columns] = (part_ref[:, columns] + value).astype(BF16)


def power_of_two(exponent):
    left = jnp.abs(exponent)
    result = jnp.ones_like(exponent)
    for bit in (64, 32, 16, 8, 4, 2, 1):
        taken = left >= bit
        step = jnp.where(exponent >= 0, 2.0**bit, 2.0**-bit)
        result = jnp.where(taken, result * step, result)
        left = jnp.where(taken, left - bit, left)
    return result


def hidden_kernel(sum_ref, out_ref):
    half = sum_ref.shape[2] // 3
    block = out_ref.shape[0]
    total = lambda part: jnp.sum(
        sum_ref[:, :, part * half : (part + 1) * half].astype(F32), axis=0
    )
    gate, up, back = total(0), total(1), total(2)
    sig = jax.nn.sigmoid(gate)
    values = (
        gate * sig * up,
        back * up * (sig * (1.0 + gate * (1.0 - sig))),
        back * (gate * sig),
    )
    lane = lax.broadcasted_iota(jnp.int32, (block, 128), 1)
    exponents = jnp.zeros(lane.shape, F32)
    place = 0
    for row in range(0, gate.shape[0], block):
        for value in values:
            value = value[row : row + block].astype(BF16).astype(F32)
            peak = jnp.max(jnp.abs(value), axis=1, keepdims=True)
            exponent = jnp.ceil(jnp.log2(jnp.maximum(peak, 2.0**-100))) - 15.0
            out_ref[:, place * half : (place + 1) * half] = (
                value * power_of_two(-exponent)
            ).astype(out_ref.dtype)
            exponents = jnp.where(lane == place, exponent, exponents)
            place += 1
    out_ref[:, place * half :] = exponents.astype(out_ref.dtype)


def products_kernel(
    all_ref, kept_ref, gate_ref, up_ref, down_ref,
    send_out, gate_out, up_out, down_out,
    hid_ref, dgate_ref, dup_ref, rows_ref, gate_sum_ref, up_sum_ref, down_sum_ref,
    sems,
):
    kept, hidden = hid_ref.shape
    half = hidden // 2
    width = gate_ref.shape[0]
    side = kept_ref.shape[1] // 2
    block = all_ref.shape[0] // 16
    strips = kept // 8 // block
    for index in range(16):
        chip, core = index // 2, index % 2
        lines = slice(index * block, (index + 1) * block)
        scale = power_of_two(all_ref[lines, 3 * strips * half :].astype(F32))
        for place in range(3 * strips):
            ref = (hid_ref, dgate_ref, dup_ref)[place % 3]
            row = (chip * strips + place // 3) * block
            ref[row : row + block, core * half : (core + 1) * half] = (
                all_ref[lines, place * half : (place + 1) * half].astype(F32)
                * scale[:, place : place + 1]
            ).astype(BF16)
    token_rows = kept_ref[:, 0:width]
    grad_rows = kept_ref[:, side : side + width]
    copies = []

    def leave(ref, out):
        copies.append(pltpu.make_async_copy(ref, out, sems.at[len(copies)]))
        copies[-1].start()

    def leave_rows(lines):
        leave(rows_ref.at[lines, :], send_out.at[lines, :])

    for ref, out, rows, values_ref in (
        (gate_sum_ref, gate_out, token_rows, dgate_ref),
        (up_sum_ref, up_out, token_rows, dup_ref),
        (down_sum_ref, down_out, grad_rows, hid_ref),
    ):
        ref[...] = mm(rows, values_ref[...], TN).astype(BF16)
        leave(ref, out)
    out_rows = mm(hid_ref[...], down_ref[...], NT).astype(BF16)
    back_rows = (
        mm(dgate_ref[...], gate_ref[...], NT) + mm(dup_ref[...], up_ref[...], NT)
    ).astype(BF16)
    pack_rows(out_rows, back_rows, rows_ref, 4, leave_rows)
    for copy in copies:
        copy.wait()


def combine_kernel(back_ref, mark_ref, scale_ref, tail_ref, mixed_ref, token_grad_ref):
    tokens, width = mixed_ref.shape
    lanes = back_ref.shape[1]
    tail = unpack_tail(back_ref[...], 2 * width - lanes)
    for ref, parts in (
        (mixed_ref, mm(scale_ref[...], back_ref[:, :width])),
        (
            token_grad_ref,
            jnp.concatenate(
                [mm(mark_ref[...], back_ref[:, width:]), mm(tail_ref[...], tail)], axis=1
            ),
        ),
    ):
        parts = parts.astype(BF16).astype(F32)
        ref[...] = (parts[0:tokens] + parts[tokens:]).astype(BF16)


def shards(tokens, expert_ids, route_weights, w_gate, w_up, w_down, grad_out):
    count, width = tokens.shape
    rep = lax.axis_size("rep")
    experts = lax.axis_size("node") * lax.axis_size("local")
    hidden = w_gate.shape[2]
    half = hidden // 2
    side = -(-width // 128) * 128
    node_hits = 2 * count // lax.axis_size("node")
    mean_count = 2 * node_hits // lax.axis_size("local")
    depth = min(mean_count + max(mean_count // 2, 1), node_hits)
    kept = experts * depth
    rows = experts * SLOTS
    lanes = 2 * width * depth // (depth + 1)
    lines = [list(range(c, rep, 2)) for c in range(2)]
    chips = rep // 2
    swap = [(i, i ^ 1) for i in range(rep)]
    core = (lax.axis_index("rep") % 2).astype(jnp.int32).reshape(1)
    gate_mat, up_mat, down_mat = w_gate[0], w_up[0], w_down[0].T

    routed = (expert_ids.T, route_weights.T, tokens, grad_out)
    send, mark, scale = call(
        route_kernel,
        [((rows, lanes), BF16), ((kept, 2 * count), BF16), ((kept, 2 * count), BF16)],
        *routed,
        far=(0, 1, 2),
        far_in=(0, 1, 2, 3),
        limit=60 * 1024 * 1024,
        scratch=[pltpu.VMEM(a.shape, a.dtype) for a in routed]
        + [pltpu.VMEM((rows, lanes), BF16)]
        + [pltpu.VMEM((kept, 2 * count), BF16)] * 2
        + [pltpu.SemaphoreType.DMA((10,))],
    )
    mine = lax.all_to_all(
        send.reshape(experts, SLOTS, lanes), ("node", "local"), 0, 0, tiled=True
    ).reshape(rows, lanes)
    packed = ((3 * width, half), BF16)
    marked = ((2 * count, rows), BF16)
    own, give, mark, scale, tail = call(
        pack_kernel,
        [packed, packed, marked, marked, ((2 * count, kept), BF16)],
        core, gate_mat, up_mat, down_mat, mark, scale,
        scalars=1,
    )
    other = lax.ppermute(give, "rep", swap)
    theirs = lax.ppermute(mine, "rep", swap)
    sums, kept_rows = call(
        own_kernel,
        [((kept, 3 * half), F32), ((kept, 2 * side), BF16)],
        mine, own,
        far=(1,),
        scratch=[pltpu.VMEM((kept, 2 * side), BF16), pltpu.SemaphoreType.DMA(())],
    )
    (sums,) = call(sums_kernel, [((kept, 3 * half), BF16)], theirs, other, sums)
    sums = lax.all_to_all(
        sums.reshape(chips, kept // chips, 3 * half),
        "rep", 0, 0, tiled=True, axis_index_groups=lines,
    )
    (piece,) = call(
        hidden_kernel, [((16, kept // chips // 16 * 3 * half + 128), BF16)], sums
    )
    piece = lax.optimization_barrier(piece.astype(jnp.float16))
    whole = lax.all_gather(piece, "rep", axis=0, tiled=True)
    whole = lax.optimization_barrier(whole).astype(BF16)
    matrix = pltpu.VMEM((kept, hidden), BF16)
    grads = ((width, hidden), BF16)
    send_back, gate_sum, up_sum, down_sum = call(
        products_kernel,
        [((rows, lanes), BF16), grads, grads, grads],
        whole, kept_rows, gate_mat, up_mat, down_mat,
        far=(0, 1, 2, 3),
        scratch=[
            matrix, matrix, matrix,
            pltpu.VMEM((rows, lanes), BF16),
            *[pltpu.VMEM(*grads)] * 3,
            pltpu.SemaphoreType.DMA((7,)),
        ],
    )
    back = lax.all_to_all(
        send_back.reshape(experts, SLOTS, lanes), ("node", "local"), 0, 0, tiled=True
    )
    mixed, token_grad = call(
        combine_kernel,
        [(tokens.shape, BF16), (tokens.shape, BF16)],
        back.reshape(rows, lanes), mark, scale, tail,
    )
    return (mixed, token_grad, gate_sum[None], up_sum[None], down_sum.T[None])


def solution(mesh):
    return jax.shard_map(
        shards,
        mesh=mesh,
        in_specs=(
            P(("node", "local"), "rep"),
            P(("node", "local"), None),
            P(("node", "local"), None),
            P(("node", "local"), "rep", None),
            P(("node", "local"), "rep", None),
            P(("node", "local"), None, "rep"),
            P(("node", "local"), "rep"),
        ),
        out_specs=(
            P(("node", "local"), "rep"),
            P(("node", "local"), "rep"),
            P(("node", "local"), "rep", None),
            P(("node", "local"), "rep", None),
            P(("node", "local"), None, "rep"),
        ),
        check_vma=False,
    )
```
